32 devices in a mesh: section: 2 (over y), dp: 2 (over x), ctx: 8 (over z, core).
Axes of the slice: x: 2, y: 2, z: 4, core: 2. Of those that a mesh axis runs over, the one named last changes fastest.
Arguments:
- inputs: bfloat16 [2, 2, 1024, 1024], P(None, 'dp', 'ctx'), may hold values from -6 to 6
- segments: int32 [2, 2, 1024], P(None, 'dp'), may hold values from 0 to 17, as said below
- cotangent: bfloat16 [2, 2, 1024, 1024], P(None, 'dp', 'ctx'), may hold values from -6 to 6
- norm_gain: bfloat16 [2, 1024], P('section', ('dp', 'ctx')), may hold values from 0.5 to 1.5
- in_weight: bfloat16 [2, 1024, 4384], P('section', ('dp', 'ctx')), may hold values from -0.1875 to 0.1875
- conv_weight: bfloat16 [2, 4, 2304], P('section', None, ('dp', 'ctx')), may hold values from -3 to 3
- conv_bias: bfloat16 [2, 2304], P('section', ('dp', 'ctx')), may hold values from -1.5 to 1.5
- dt_bias: float32 [2, 32], P('section'), may hold values from -0.5 to 1.5
- a_log: float32 [2, 32], P('section'), as said below
- skip_gain: float32 [2, 32], P('section'), may hold values from 0.5 to 1.5
- gate_gain: bfloat16 [2, 2048], P('section', ('dp', 'ctx')), may hold values from 0.5 to 1.5
- out_weight: bfloat16 [2, 2048, 1024], P('section', ('dp', 'ctx')), may hold values from -0.125 to 0.125
Outputs:
- section_ends: float32 [2, 2, 2, 1024, 1024], P('section', None, 'dp', 'ctx')
- grad_norm_gain: float32 [2, 1024], P('section', ('dp', 'ctx'))
- grad_in_weight: float32 [2, 1024, 4384], P('section', ('dp', 'ctx'))
- grad_conv_weight: float32 [2, 4, 2304], P('section', None, ('dp', 'ctx'))
- grad_conv_bias: float32 [2, 2304], P('section', ('dp', 'ctx'))
- grad_dt_bias: float32 [2, 32], P('section')
- grad_a_log: float32 [2, 32], P('section')
- grad_skip_gain: float32 [2, 32], P('section')
- grad_gate_gain: float32 [2, 2048], P('section', ('dp', 'ctx'))
- grad_out_weight: float32 [2, 2048, 1024], P('section', ('dp', 'ctx'))
The draws below stay inside these ranges and needn't reach their ends.
Inputs may be any that keep to these rules, and one draw needn't show every extreme that they name: `segments`: each sequence's document numbers start at 0, never fall and rise by one where a document starts; documents hold 60 to 800 tokens, except the last of a sequence, which may be shorter, and a sequence's single document, which holds all its tokens; for each sequence index, one micro-batch drawn from the seed holds a single document over the whole sequence; some sequence reaches the largest document number. exp(a_log) lies between 0.2 / 1024 and 0.04.
All inputs are finite; a program needn't handle non-finite values.
Results may differ from the reference program's by a relative error of at most 0.013.
Values may be sent and summed in bfloat16 or wider, within the bound.
A program may use at most 192 MiB of HBM per device.

```python
import math
import jax
import jax.numpy as jnp
from jax import lax

D = 1024
DI = 2048
HEADS = 32
HEAD = 64
STATE = 128
CONV = 4
MB = 2
DOC_MIN = 60
DOC_MAX = 800
LAYERS = 2
SEQS = 2
SEQ_LEN = 1024
XBC = 2304
PROJ = 4384


def draw_segments(key, part):
    key = jax.random.fold_in(key, 5)
    length_key, whole_key = jax.random.split(key)
    count_docs = SEQ_LEN // DOC_MIN + 1
    doc_lengths = jax.random.randint(length_key, (MB, SEQS, count_docs), DOC_MIN, DOC_MAX + 1)
    doc_ends = jnp.cumsum(doc_lengths, axis=-1)
    positions = jnp.arange(SEQ_LEN)
    numbers = jnp.sum((doc_ends[:, :, None, :] <= positions[None, None, :, None]).astype(jnp.int32), axis=-1)
    chosen = jax.random.randint(whole_key, (SEQS,), 0, MB)
    dense_micro = (chosen[0] + 1) % MB
    dense_mask = (jnp.arange(MB)[:, None] == dense_micro) & (jnp.arange(SEQS)[None, :] == 0)
    dense_numbers = (positions // DOC_MIN).astype(jnp.int32)
    numbers = jnp.where(dense_mask[:, :, None], dense_numbers[None, None, :], numbers)
    single = jnp.arange(MB)[:, None] == chosen[None, :]
    return jnp.where(single[:, :, None], 0, numbers).astype(jnp.int32)


def draw_a_log(key, part):
    key = jax.random.fold_in(key, 7)
    pick_key, slow_key, fast_key = jax.random.split(key, 3)
    slow_rate = jnp.exp(jax.random.uniform(slow_key, (LAYERS, HEADS), jnp.float32, math.log(0.2 / SEQ_LEN), math.log(1.5 / SEQ_LEN)))
    fast_rate = jnp.exp(jax.random.uniform(fast_key, (LAYERS, HEADS), jnp.float32, math.log(1.0 / 60.0), math.log(1.0 / 25.0)))
    slow_mask = jax.random.uniform(pick_key, (LAYERS, HEADS), jnp.float32) < 0.5
    return jnp.log(jnp.where(slow_mask, slow_rate, fast_rate)).astype(jnp.float32)


def level_of(own_key, dims, shards, least, largest):
    level, own = 1.0, jax.random.fold_in(own_key, 6)
    for position, parts in shards:
        draws = jnp.exp(jax.random.uniform(jax.random.fold_in(own, position), (parts,), jnp.float32, least / len(shards), largest / len(shards)))
        level = level * jnp.repeat(draws, dims[position] // parts).reshape([-1 if axis == position else 1 for axis in range(len(dims))])
    return level


def centred(own_key, shape, width, most, pieces=(), kind=jnp.bfloat16):
    entries = width * jax.random.normal(own_key, shape, jnp.float32)
    if pieces:
        entries = entries * level_of(own_key, shape, pieces, -0.22, 0.18)
    return jnp.clip(entries, -most, most).astype(kind)


def setup_inputs(seed: int = 0) -> dict:
    streams_of = jax.random.split(jax.random.key(seed), 13)
    return {
        "inputs": centred(streams_of[0], (MB, SEQS, SEQ_LEN, D), 1.0, 6.0, ((1, 2), (2, 8))),
        "segments": draw_segments(jax.random.fold_in(streams_of[12], 71), 0),
        "cotangent": centred(streams_of[2], (MB, SEQS, SEQ_LEN, D), 1.0, 6.0, ((1, 2), (2, 8))),
        "norm_gain": jnp.clip(1.0 + 0.1 * jax.random.normal(streams_of[3], (LAYERS, D), jnp.float32), 0.5, 1.5).astype(jnp.bfloat16),
        "in_weight": centred(streams_of[4], (LAYERS, D, PROJ), D ** -0.5, 0.1875, ((0, 2), (1, 16))),
        "conv_weight": centred(streams_of[5], (LAYERS, CONV, XBC), CONV ** -0.5, 3.0, ((0, 2), (2, 16))),
        "conv_bias": centred(streams_of[6], (LAYERS, XBC), 0.3, 1.5, ((0, 2), (1, 16))),
        "dt_bias": jnp.clip(-0.5 + 2.0 * jax.random.uniform(streams_of[7], (LAYERS, HEADS), jnp.float32) ** level_of(streams_of[7], (LAYERS, HEADS), ((0, 2),), -0.2, 0.2), -0.5, 1.5),
        "a_log": draw_a_log(jax.random.fold_in(streams_of[12], 71), 0),
        "skip_gain": jnp.clip(0.5 + 1.0 * jax.random.uniform(streams_of[9], (LAYERS, HEADS), jnp.float32) ** level_of(streams_of[9], (LAYERS, HEADS), ((0, 2),), -0.2, 0.2), 0.5, 1.5),
        "gate_gain": jnp.clip(1.0 + 0.1 * jax.random.normal(streams_of[10], (LAYERS, DI), jnp.float32), 0.5, 1.5).astype(jnp.bfloat16),
        "out_weight": centred(streams_of[11], (LAYERS, DI, D), DI ** -0.5, 0.125, ((0, 2), (1, 16))),
    }


EPS = 1e-05
HIGH = lax.Precision.HIGHEST

@jax.custom_vjp
def low(v):
    return lax.optimization_barrier(v.astype(jnp.bfloat16)).astype(jnp.float32)

@jax.custom_vjp
def low_back(v):
    return v

def low_keep(v):
    return (low(v), None)

def low_pass(kept, grad):
    return (grad,)

def back_keep(v):
    return (v, None)

def back_low(kept, grad):
    return (low(grad),)
low.defvjp(low_keep, low_pass)
low_back.defvjp(back_keep, back_low)

def rms_scale(values):
    return values * lax.rsqrt(lax.optimization_barrier(jnp.mean(values * values, axis=-1, keepdims=True)) + EPS)

def norm_in(values, gain_vec):
    return rms_scale(values) * gain_vec

def conv_part(extended, seg_ext, conv_taps, conv_offset):
    taps_count = conv_taps.shape[0]
    length = extended.shape[0] - (taps_count - 1)
    current = seg_ext[taps_count - 1:]
    summed = conv_offset + conv_taps[0] * extended[taps_count - 1:]
    for offset in range(1, taps_count):
        begin_at = taps_count - 1 - offset
        shifted = extended[begin_at:begin_at + length]
        matches = seg_ext[begin_at:begin_at + length] == current
        summed = summed + conv_taps[offset] * jnp.where(matches[:, None], shifted, 0.0)
    return jax.nn.silu(summed)

def mixer_front(extended, step_raw, conv_taps, conv_offset, step_shift, a_logs, seg_ext):
    conved = conv_part(extended, seg_ext, conv_taps, conv_offset)
    inner_vals = conved[:, :DI].reshape(conved.shape[0], HEADS, HEAD)
    write_vec = conved[:, DI:DI + STATE]
    read_vec = conved[:, DI + STATE:]
    step_size = jax.nn.softplus(step_raw + step_shift)
    log_decay = -step_size * jnp.exp(a_logs)
    return (inner_vals, write_vec, read_vec, step_size, log_decay)

def block_summary(inner_vals, write_vec, step_size, log_decay, seg_block, seg_prior):
    cum_decay = jnp.cumsum(log_decay, axis=0)
    in_last = seg_block == seg_block[-1]
    tail_weight = jnp.where(in_last[:, None], jnp.exp(cum_decay[-1][None, :] - cum_decay), 0.0) * step_size
    local_state = jnp.einsum('shp,sn->hpn', tail_weight[:, :, None] * inner_vals, write_vec, precision=HIGH)
    decay_tot = jnp.where(seg_block[-1] == seg_prior, jnp.exp(cum_decay[-1]), 0.0)
    return (decay_tot, local_state)

def block_output(inner_vals, write_vec, read_vec, step_size, log_decay, seg_block, seg_prior, skip_vec, state_in):
    cum_decay = jnp.cumsum(log_decay, axis=0)
    block_len = seg_block.shape[0]
    order_idx = jnp.arange(block_len)
    same_doc = (seg_block[:, None] == seg_block[None, :]) & (order_idx[None, :] <= order_idx[:, None])
    rate_rows = cum_decay.T
    decay_mat = jnp.exp(jnp.where(same_doc[None], rate_rows[:, :, None] - rate_rows[:, None, :], -jnp.inf))
    scores = jnp.dot(read_vec, write_vec.T, precision=HIGH)
    weights = decay_mat * scores[None] * step_size.T[:, None, :]
    mixed_vals = jnp.einsum('hts,shp->thp', weights, inner_vals, precision=HIGH)
    carry_in = jnp.where((seg_block == seg_prior)[:, None], jnp.exp(cum_decay), 0.0)
    mixed_vals = mixed_vals + carry_in[:, :, None] * jnp.einsum('hpn,tn->thp', state_in, read_vec, precision=HIGH)
    return mixed_vals + skip_vec[None, :, None] * inner_vals

def layer_apply(values, seg_seq, params):
    gain_in, in_mat, conv_taps, conv_offset, step_shift, a_logs, skip_vec, gain_gate, out_mat = params
    length = values.shape[0]
    taps_count = conv_taps.shape[0]
    normed = low(norm_in(values, gain_in))
    projected = low_back(jnp.dot(normed, in_mat, precision=HIGH))
    gate_vals = projected[:, :DI]
    conv_in = low(projected[:, DI:DI + XBC])
    step_raw = projected[:, DI + XBC:]
    seg_ext = jnp.concatenate([jnp.full((taps_count - 1,), -1, jnp.int32), seg_seq.astype(jnp.int32)])
    extended = jnp.concatenate([jnp.zeros((taps_count - 1, XBC), jnp.float32), conv_in], axis=0)
    inner_vals, write_vec, read_vec, step_size, log_decay = mixer_front(extended, step_raw, conv_taps, conv_offset, step_shift, a_logs, seg_ext)
    block_size = math.gcd(length, 256)
    count_blocks = length // block_size
    priors = seg_ext[taps_count - 2:taps_count - 2 + length][::block_size]

    def reshape_blocks(array_vals):
        return array_vals.reshape((count_blocks, block_size) + array_vals.shape[1:])

    def advance(state_vals, block_item):
        inner_block, write_block, read_block, step_block, decay_block, seg_block, prior_block = block_item
        decay_tot, local_state = block_summary(inner_block, write_block, step_block, decay_block, seg_block, prior_block)
        mixed_block = block_output(inner_block, write_block, read_block, step_block, decay_block, seg_block, prior_block, skip_vec, state_vals)
        return (decay_tot[:, None, None] * state_vals + local_state, mixed_block)
    block_items = (reshape_blocks(inner_vals), reshape_blocks(write_vec), reshape_blocks(read_vec), reshape_blocks(step_size), reshape_blocks(log_decay), reshape_blocks(seg_seq.astype(jnp.int32)), priors)
    start_state = jnp.zeros((HEADS, HEAD, STATE), jnp.float32)
    unused, mixed_out = lax.scan(jax.checkpoint(advance), start_state, block_items)
    gated = mixed_out.reshape(length, DI) * jax.nn.silu(gate_vals)
    normed_out = low(norm_in(gated, gain_gate))
    branch = low_back(jnp.dot(normed_out, out_mat, precision=HIGH))
    return values + branch

def reference(inputs, segments, cotangent, norm_gain, in_weight, conv_weight, conv_bias, dt_bias, a_log, skip_gain, gate_gain, out_weight):
    params = tuple((param_arr.astype(jnp.float32) for param_arr in (norm_gain, in_weight, conv_weight, conv_bias, dt_bias, a_log, skip_gain, gate_gain, out_weight)))
    flat_segments = segments.reshape(MB * SEQS, SEQ_LEN).astype(jnp.int32)

    def forward(values, *layer_params):
        first_params = tuple((weight_arr[0] for weight_arr in layer_params))
        second_params = tuple((weight_arr[1] for weight_arr in layer_params))

        def per_sequence(carry_val, seq_item):
            seq_vals, seg_seq = seq_item
            middle = low_back(low(layer_apply(seq_vals, seg_seq, first_params)))
            return (carry_val, layer_apply(middle, seg_seq, second_params))
        unused, outputs = lax.scan(jax.checkpoint(per_sequence), jnp.float32(0.0), (values.reshape(MB * SEQS, SEQ_LEN, D), flat_segments))
        return outputs.reshape(values.shape)
    outputs, pull_back = jax.vjp(forward, inputs.astype(jnp.float32), *params)
    gradients = pull_back(cotangent.astype(jnp.float32))
    section_ends = jnp.stack([gradients[0], outputs])
    return (section_ends, gradients[1], gradients[2], gradients[3], gradients[4], gradients[5], gradients[6], gradients[7], gradients[8], gradients[9])
```

```python
import jax
import jax.numpy as jnp
from jax import lax
from jax.sharding import PartitionSpec as P

DI = 2048
HEADS = 32
HEAD = 64
STATE = 128
XBC = 2304
PROJ = 4384


EPS = 1e-05
HIGH = lax.Precision.HIGHEST


def passed_along(block, axis, distance):
    devices = range(lax.axis_size(axis))
    route = [(i - distance, i) for i in devices if i - distance in devices]
    return lax.ppermute(block, axis, route)


def rms_scale(values):
    return values * lax.rsqrt(jnp.mean(values * values, axis=-1, keepdims=True) + EPS)


def norm_in(values, gain_vec):
    return rms_scale(values) * gain_vec


def conv_part(extended, seg_ext, conv_taps, conv_offset):
    taps_count = conv_taps.shape[0]
    length = extended.shape[0] - (taps_count - 1)
    current = seg_ext[taps_count - 1 :]
    summed = conv_offset + conv_taps[0] * extended[taps_count - 1 :]
    for offset in range(1, taps_count):
        begin_at = taps_count - 1 - offset
        shifted = extended[begin_at : begin_at + length]
        matches = seg_ext[begin_at : begin_at + length] == current
        summed = summed + conv_taps[offset] * jnp.where(matches[:, None], shifted, 0.0)
    return jax.nn.silu(summed)


def mixer_front(extended, step_raw, conv_taps, conv_offset, step_shift, a_logs, seg_ext):
    conved = conv_part(extended, seg_ext, conv_taps, conv_offset)
    inner_vals = conved[:, :DI].reshape(conved.shape[0], HEADS, HEAD)
    write_vec = conved[:, DI : DI + STATE]
    read_vec = conved[:, DI + STATE :]
    step_size = jax.nn.softplus(step_raw + step_shift)
    log_decay = -step_size * jnp.exp(a_logs)
    return (inner_vals, write_vec, read_vec, step_size, log_decay)


def block_summary(inner_vals, write_vec, step_size, log_decay, seg_block, seg_prior):
    cum_decay = jnp.cumsum(log_decay, axis=0)
    in_last = seg_block == seg_block[-1]
    tail_weight = (
        jnp.where(in_last[:, None], jnp.exp(cum_decay[-1][None, :] - cum_decay), 0.0) * step_size
    )
    local_state = jnp.einsum(
        "shp,sn->hpn", tail_weight[:, :, None] * inner_vals, write_vec, precision=HIGH
    )
    decay_tot = jnp.where(seg_block[-1] == seg_prior, jnp.exp(cum_decay[-1]), 0.0)
    return (decay_tot, local_state)


def block_output(
    inner_vals, write_vec, read_vec, step_size, log_decay, seg_block, seg_prior, skip_vec, state_in
):
    cum_decay = jnp.cumsum(log_decay, axis=0)
    block_len = seg_block.shape[0]
    order_idx = jnp.arange(block_len)
    same_doc = (seg_block[:, None] == seg_block[None, :]) & (
        order_idx[None, :] <= order_idx[:, None]
    )
    rate_rows = cum_decay.T
    decay_mat = jnp.exp(
        jnp.where(same_doc[None], rate_rows[:, :, None] - rate_rows[:, None, :], -jnp.inf)
    )
    scores = jnp.dot(read_vec, write_vec.T, precision=HIGH)
    weights = decay_mat * scores[None] * step_size.T[:, None, :]
    mixed_vals = jnp.einsum("hts,shp->thp", weights, inner_vals, precision=HIGH)
    carry_in = jnp.where((seg_block == seg_prior)[:, None], jnp.exp(cum_decay), 0.0)
    mixed_vals = mixed_vals + carry_in[:, :, None] * jnp.einsum(
        "hpn,tn->thp", state_in, read_vec, precision=HIGH
    )
    return mixed_vals + skip_vec[None, :, None] * inner_vals


def gated_output(
    inner_vals,
    write_vec,
    read_vec,
    step_size,
    log_decay,
    gate_vals,
    skip_vec,
    gain_gate,
    state_in,
    seg_block,
    seg_prior,
):
    mixed_vals = block_output(
        inner_vals,
        write_vec,
        read_vec,
        step_size,
        log_decay,
        seg_block,
        seg_prior,
        skip_vec,
        state_in,
    )
    gated = mixed_vals.reshape(mixed_vals.shape[0], DI) * jax.nn.silu(gate_vals)
    return norm_in(gated, gain_gate)


def split_three(values):
    high = lax.reduce_precision(values, 8, 7)
    rest = values - high
    middle = lax.reduce_precision(rest, 8, 7)
    last = lax.reduce_precision(rest - middle, 8, 7)
    return [part.astype(jnp.bfloat16) for part in (high, middle, last)]


def chain_weights(decays, me, step):
    count = decays.shape[0]
    running = jnp.ones(decays.shape[1:], jnp.float32)
    order = range(count - 1, -1, -1) if step > 0 else range(count)
    found = [None] * count
    for block in order:
        ahead = block < me if step > 0 else block > me
        found[block] = jnp.where(ahead, running, 0.0)
        running = jnp.where(ahead, running * decays[block], running)
    return jnp.stack(found)


def gather_states(decay_tot, local_state):
    heads, channels, width = local_state.shape
    row = jnp.concatenate(split_three(decay_tot))
    row = jnp.pad(row, (0, width - row.shape[0]))[None]
    row = jnp.pad(row, ((0, 15), (0, 0)))
    rows = jnp.concatenate([local_state.reshape(heads * channels, width).astype(jnp.bfloat16), row])
    every = lax.all_gather(rows, "ctx", axis=0, tiled=False)
    coded = every[:, heads * channels, : 3 * heads].astype(jnp.float32)
    decays = coded[:, :heads] + (coded[:, heads : 2 * heads] + coded[:, 2 * heads :])
    factors = chain_weights(decays, lax.axis_index("ctx"), 1)
    states = every[:, : heads * channels].reshape(-1, heads, channels, width)
    return decays, jnp.sum(factors[:, :, None, None] * states.astype(jnp.float32), axis=0)


def gather_grads(decays, direct):
    heads, channels, width = direct.shape
    rows = direct.reshape(heads * channels, width).astype(jnp.bfloat16)
    every = lax.all_gather(rows, "ctx", axis=0, tiled=False)
    factors = chain_weights(decays, lax.axis_index("ctx"), -1)
    states = every.reshape(-1, heads, channels, width)
    return jnp.sum(factors[:, :, None, None] * states.astype(jnp.float32), axis=0)


def pack_small(pieces, width):
    packed = jnp.concatenate(pieces, axis=-1)
    return jnp.pad(packed, [(0, 0)] * (packed.ndim - 1) + [(0, width - packed.shape[-1])])


def body(
    inputs,
    segments,
    cotangent,
    norm_gain,
    in_weight,
    conv_weight,
    conv_bias,
    dt_bias,
    a_log,
    skip_gain,
    gate_gain,
    out_weight,
):
    section_index = lax.axis_index("section")
    ctx_index = lax.axis_index("ctx")
    micro_count = inputs.shape[0]
    tokens = inputs.shape[2]
    model_width = inputs.shape[3]
    taps_count = conv_weight.shape[1]
    step_shift = dt_bias[0]
    a_logs = a_log[0]
    skip_vec = skip_gain[0]

    both = ("dp", "ctx")
    shards = lax.axis_size("dp") * lax.axis_size("ctx")
    gain_len, gate_len = norm_gain.shape[1], gate_gain.shape[1]
    conv_len = conv_bias.shape[1]
    small_len = gain_len + gate_len + (taps_count + 1) * conv_len
    small_width = -(-small_len // 1024) * 1024
    own_small = pack_small(
        [norm_gain[0], gate_gain[0], conv_bias[0], conv_weight[0].reshape(-1)], small_width
    )
    small_all = lax.all_gather(
        own_small.reshape(small_width // 128, 128), both, axis=0, tiled=True
    )
    small_all = small_all.reshape(shards, small_width).astype(jnp.float32)
    marks = (gain_len, gain_len + gate_len, gain_len + gate_len + conv_len, small_len)
    all_taps = small_all[:, marks[2] : marks[3]].reshape(shards, taps_count, conv_len)
    weights = (
        small_all[:, : marks[0]].reshape(-1),
        lax.all_gather(in_weight, both, axis=1, tiled=True)[0],
        jnp.transpose(all_taps, (1, 0, 2)).reshape(taps_count, -1),
        small_all[:, marks[1] : marks[2]].reshape(-1),
        small_all[:, marks[0] : marks[1]].reshape(-1),
        lax.all_gather(out_weight, both, axis=1, tiled=True)[0],
    )
    padded = jnp.concatenate(
        [jnp.full((micro_count, taps_count - 1), -1, jnp.int32), segments[:, 0]], axis=1
    )

    def layer_backward(grad_next, saved, is_active, layer_weights):
        gain_in, in_mat, conv_taps, conv_offset, gain_gate, out_mat = layer_weights
        layer_in, normed, projected, extended, state_in, mixed_out, seg_ext, decays = saved
        seg_block = seg_ext[taps_count - 1 :]
        seg_prior = seg_ext[taps_count - 2]
        grad_out = jnp.where(is_active, grad_next, 0.0).astype(jnp.bfloat16)
        grad_mixed = lax.cond(
            is_active,
            lambda: lax.dot_general(
                grad_out, out_mat, (((1,), (1,)), ((), ())), preferred_element_type=jnp.float32
            ),
            lambda: jnp.zeros((tokens, DI), jnp.float32),
        )
        gate_vals = projected[:, :DI]
        step_raw = projected[:, DI + XBC :]

        def front_local(ext_vals, raw_vals, taps_vals, offset_vals, shift_vals, log_vals):
            return mixer_front(
                ext_vals, raw_vals, taps_vals, offset_vals, shift_vals, log_vals, seg_ext
            )

        pieces, front_pull = jax.vjp(
            front_local,
            extended.astype(jnp.float32),
            step_raw,
            conv_taps,
            conv_offset,
            step_shift,
            a_logs,
        )

        def output_local(
            inner_vals,
            write_vec,
            read_vec,
            step_size,
            log_decay,
            gate_part,
            skip_part,
            gain_part,
            state_part,
        ):
            return gated_output(
                inner_vals,
                write_vec,
                read_vec,
                step_size,
                log_decay,
                gate_part,
                skip_part,
                gain_part,
                state_part,
                seg_block,
                seg_prior,
            )

        unused_out, output_pull = jax.vjp(
            output_local,
            pieces[0],
            pieces[1],
            pieces[2],
            pieces[3],
            pieces[4],
            gate_vals,
            skip_vec,
            gain_gate,
            state_in,
        )
        (
            grad_inner,
            grad_write,
            grad_read,
            grad_step,
            grad_logdec,
            grad_gate,
            grad_skip,
            grad_gaingate,
            grad_state,
        ) = output_pull(grad_mixed)

        def summary_local(inner_vals, write_vec, step_size, log_decay):
            return block_summary(inner_vals, write_vec, step_size, log_decay, seg_block, seg_prior)

        summary_vals, summary_pull = jax.vjp(
            summary_local, pieces[0], pieces[1], pieces[3], pieces[4]
        )
        onward = gather_grads(decays, grad_state)
        back_inner, back_write, back_step, back_logdec = summary_pull(
            (jnp.sum(onward * state_in, axis=(1, 2)), onward)
        )
        grad_ext, grad_raw, grad_taps, grad_offset, grad_shift, grad_alog = front_pull(
            (
                grad_inner + back_inner,
                grad_write + back_write,
                grad_read,
                grad_step + back_step,
                grad_logdec + back_logdec,
            )
        )
        returned = passed_along(grad_ext[: taps_count - 1], "ctx", -1)
        grad_conv = grad_ext[taps_count - 1 :] + jnp.concatenate(
            [jnp.zeros((tokens - taps_count + 1, XBC), jnp.float32), returned], axis=0
        )
        grad_proj = jnp.where(
            is_active, jnp.concatenate([grad_gate, grad_conv, grad_raw], axis=1), 0.0
        ).astype(jnp.bfloat16)
        grad_normed = lax.cond(
            is_active,
            lambda: lax.dot_general(
                grad_proj, in_mat, (((1,), (1,)), ((), ())), preferred_element_type=jnp.float32
            ),
            lambda: jnp.zeros((tokens, model_width), jnp.float32),
        )
        unused_norm, norm_pull = jax.vjp(norm_in, layer_in.astype(jnp.float32), gain_in)
        grad_layer, grad_gainin = norm_pull(grad_normed)
        small_grads = (grad_gainin, grad_taps, grad_offset, grad_gaingate)
        return (
            grad_next + grad_layer,
            small_grads,
            (grad_shift, grad_alog, grad_skip),
            (normed, grad_proj, mixed_out, grad_out),
        )

    received = jnp.zeros((tokens, model_width), jnp.bfloat16)
    results = []
    kept_all = []
    for tick_index in range(micro_count + 1):
        own_input = inputs[min(tick_index, micro_count - 1), 0]
        layer_in = jnp.where(section_index == 0, own_input, received)
        micro_index = jnp.clip(tick_index - section_index, 0, micro_count - 1)
        is_active = jnp.where(section_index == 0, tick_index < micro_count, tick_index >= 1)
        seg_row = lax.dynamic_index_in_dim(padded, micro_index, 0, keepdims=False)
        layer_seg_ext = lax.dynamic_slice_in_dim(
            seg_row, ctx_index * tokens, tokens + taps_count - 1
        )
        (
            layer_gain_in,
            layer_in_mat,
            layer_conv_taps,
            layer_conv_offset,
            layer_gain_gate,
            layer_out_mat,
        ) = weights
        layer_seg_block = layer_seg_ext[taps_count - 1 :]
        layer_seg_prior = layer_seg_ext[taps_count - 2]
        start_vals = layer_in.astype(jnp.float32)
        layer_normed = norm_in(start_vals, layer_gain_in).astype(jnp.bfloat16)
        layer_projected = lax.cond(
            is_active,
            lambda: jnp.dot(layer_normed, layer_in_mat, preferred_element_type=jnp.float32),
            lambda: jnp.zeros((tokens, PROJ), jnp.float32),
        )
        layer_gate_vals = layer_projected[:, :DI]
        raw_conv = layer_projected[:, DI : DI + XBC].astype(jnp.bfloat16)
        layer_step_raw = layer_projected[:, DI + XBC :]
        before = passed_along(raw_conv[tokens - taps_count + 1 :], "ctx", 1)
        layer_extended = jnp.concatenate([before, raw_conv], axis=0)
        layer_pieces = mixer_front(
            layer_extended.astype(jnp.float32),
            layer_step_raw,
            layer_conv_taps,
            layer_conv_offset,
            step_shift,
            a_logs,
            layer_seg_ext,
        )
        decay_tot, local_state = block_summary(
            layer_pieces[0],
            layer_pieces[1],
            layer_pieces[3],
            layer_pieces[4],
            layer_seg_block,
            layer_seg_prior,
        )
        decays_all, layer_state_in = gather_states(decay_tot, local_state)
        layer_mixed_out = gated_output(
            layer_pieces[0],
            layer_pieces[1],
            layer_pieces[2],
            layer_pieces[3],
            layer_pieces[4],
            layer_gate_vals,
            skip_vec,
            layer_gain_gate,
            layer_state_in,
            layer_seg_block,
            layer_seg_prior,
        ).astype(jnp.bfloat16)
        branch = lax.cond(
            is_active,
            lambda: jnp.dot(layer_mixed_out, layer_out_mat, preferred_element_type=jnp.float32),
            lambda: jnp.zeros((tokens, model_width), jnp.float32),
        )
        result = start_vals + branch
        saved = (
            layer_in,
            layer_normed,
            layer_projected,
            layer_extended,
            layer_state_in,
            layer_mixed_out,
            layer_seg_ext,
            decays_all,
        )
        results.append(result)
        kept_all.append(saved)
        if tick_index < micro_count:
            received = passed_along(result.astype(jnp.bfloat16), "section", 1)
    small_sums = (
        jnp.zeros(weights[0].shape, jnp.float32),
        jnp.zeros(weights[2].shape, jnp.float32),
        jnp.zeros(weights[3].shape, jnp.float32),
        jnp.zeros(weights[4].shape, jnp.float32),
    )
    head_sums = tuple((jnp.zeros(step_shift.shape, jnp.float32) for repeat_idx in range(3)))
    returned_grad = jnp.zeros((tokens, model_width), jnp.bfloat16)
    grad_inputs = []
    row_parts = []
    for tick_index in range(micro_count + 1):
        lower_saved = kept_all[max(tick_index - 1, 0)]
        upper_saved = kept_all[min(tick_index + 1, micro_count)]
        saved = jax.tree.map(
            lambda lower_val, upper_val: jnp.where(section_index == 0, lower_val, upper_val),
            lower_saved,
            upper_saved,
        )
        target = cotangent[min(tick_index, micro_count - 1), 0].astype(jnp.float32)
        grad_next = jnp.where(section_index == 1, target, returned_grad.astype(jnp.float32))
        is_active = jnp.where(section_index == 1, tick_index < micro_count, tick_index >= 1)
        grad_input, small_grads, head_grads, rows_kept = layer_backward(
            grad_next, saved, is_active, weights
        )
        small_sums = jax.tree.map(
            lambda running, update: running + jnp.where(is_active, update, 0.0),
            small_sums,
            small_grads,
        )
        head_sums = jax.tree.map(
            lambda running, update: running + jnp.where(is_active, update, 0.0),
            head_sums,
            head_grads,
        )
        row_parts.append(rows_kept)
        grad_inputs.append(grad_input)
        if tick_index < micro_count:
            returned_grad = passed_along(grad_input.astype(jnp.bfloat16), "section", -1)
    normed_rows = jnp.concatenate([part_item[0] for part_item in row_parts], axis=0)
    proj_rows = jnp.concatenate([part_item[1] for part_item in row_parts], axis=0)
    mixed_rows = jnp.concatenate([part_item[2] for part_item in row_parts], axis=0)
    branch_rows = jnp.concatenate([part_item[3] for part_item in row_parts], axis=0)
    proj_width = proj_rows.shape[1]
    proj_rows = jnp.pad(proj_rows, ((0, 0), (0, -proj_width % 128)))
    grad_outmat = lax.dot_general(
        mixed_rows, branch_rows, (((0,), (0,)), ((), ())), preferred_element_type=jnp.float32
    ).astype(jnp.bfloat16)
    grad_inmat = lax.dot_general(
        normed_rows, proj_rows, (((0,), (0,)), ((), ())), preferred_element_type=jnp.float32
    ).astype(jnp.bfloat16)
    own_outmat = lax.psum_scatter(grad_outmat, both, scatter_dimension=0, tiled=True)
    own_inmat = lax.psum_scatter(grad_inmat, both, scatter_dimension=0, tiled=True)
    taps_turned = small_sums[1].reshape(taps_count, shards, conv_len)
    sums_len = small_len + 3 * a_logs.shape[0]
    sums_width = -(-sums_len // 1024) * 1024
    heads_row = jnp.concatenate(head_sums)
    sums_rows = pack_small(
        [
            small_sums[0].reshape(shards, gain_len),
            small_sums[3].reshape(shards, gate_len),
            small_sums[2].reshape(shards, conv_len),
            jnp.transpose(taps_turned, (1, 0, 2)).reshape(shards, -1),
            jnp.broadcast_to(heads_row[None], (shards, heads_row.shape[0])),
        ],
        sums_width,
    ).reshape(shards * (sums_width // 128), 128)
    own_sums = lax.psum_scatter(sums_rows, both, scatter_dimension=0, tiled=True).reshape(-1)
    head_totals = own_sums[small_len:sums_len].reshape(3, 1, -1)
    ends_rows = [
        jnp.where(section_index == 0, grad_inputs[micro_index + 1], results[micro_index + 1])
        for micro_index in range(micro_count)
    ]
    section_ends = jnp.stack(ends_rows)[None, :, None]
    return (
        section_ends,
        own_sums[None, : marks[0]],
        own_inmat[None, :, :proj_width].astype(jnp.float32),
        own_sums[marks[2] : marks[3]].reshape(1, taps_count, conv_len),
        own_sums[None, marks[1] : marks[2]],
        head_totals[0],
        head_totals[1],
        head_totals[2],
        own_sums[None, marks[0] : marks[1]],
        own_outmat[None].astype(jnp.float32),
    )


def solution(mesh):
    return jax.shard_map(
        body,
        mesh=mesh,
        in_specs=(
            P(None, "dp", "ctx", None),
            P(None, "dp", None),
            P(None, "dp", "ctx", None),
            P("section", ("dp", "ctx")),
            P("section", ("dp", "ctx"), None),
            P("section", None, ("dp", "ctx")),
            P("section", ("dp", "ctx")),
            P("section", None),
            P("section", None),
            P("section", None),
            P("section", ("dp", "ctx")),
            P("section", ("dp", "ctx"), None),
        ),
        out_specs=(
            P("section", None, "dp", "ctx", None),
            P("section", ("dp", "ctx")),
            P("section", ("dp", "ctx"), None),
            P("section", None, ("dp", "ctx")),
            P("section", ("dp", "ctx")),
            P("section", None),
            P("section", None),
            P("section", None),
            P("section", ("dp", "ctx")),
            P("section", ("dp", "ctx"), None),
        ),
        check_vma=False,
    )
```
